32 devices in a mesh: groups: 2 (over y), seq: 4 (over z), head: 4 (over x, core).
Axes of the slice: x: 2, y: 2, z: 4, core: 2. Of those that a mesh axis runs over, the one named last changes fastest.
Arguments:
- queries: bfloat16 [4096, 2048], P(('groups', 'seq'), 'head'), parts along dimension 0, may hold values from -6 to 6
- keys: bfloat16 [4096, 2048], P(('groups', 'seq'), 'head'), parts along dimension 0, may hold values from -6 to 6
- values: bfloat16 [4096, 2048], P(('groups', 'seq'), 'head'), parts along dimension 0, may hold values from -6 to 6
- cotangent: bfloat16 [4096, 2048], P(('groups', 'seq'), 'head'), parts along dimension 0, may hold values from -6 to 6
- cluster_ids: int32 [2048, 1], P(('groups', 'seq')), parts along dimension 0, may hold values from 0 to 7; in each aligned block of 256 rows (0 to 255, 256 to 511, ...) at most 96 rows name the same one
- centroids: float32 [8, 2048], P(None, 'head'), may hold values from -0.6 to 0.6
Outputs:
- attended: bfloat16 [4096, 2048], P(('groups', 'seq'), 'head'), parts along dimension 0
- grad_queries: bfloat16 [4096, 2048], P(('groups', 'seq'), 'head'), parts along dimension 0
- grad_keys: bfloat16 [4096, 2048], P(('groups', 'seq'), 'head'), parts along dimension 0
- grad_values: bfloat16 [4096, 2048], P(('groups', 'seq'), 'head'), parts along dimension 0
- new_centroids: float32 [16, 2048], P('groups', 'head'), parts along dimension 0
The draws below stay inside these ranges and needn't reach their ends.
There are 2 independent parts, one for each index of `groups`. The reference program is written for one: setup_inputs(seed, part) draws one part's arguments, and reference() takes and returns one part's arrays. A program takes and returns all parts, laid end to end along the dimension named above; an argument that names none is the same for every part. Nothing has to cross between parts.
Inputs may be any that keep to these rules, and one draw needn't show every extreme that they name: `cluster_ids`: tokens 2m and 2m+1 take the cluster of pair m. Among the 256 pairs of one index of seq no cluster is named more than 96 times, and some cluster is named exactly that often; every cluster is named by some pair.
All inputs are finite; a program needn't handle non-finite values.
Results may differ from the reference program's by a relative error of at most 0.02.
Values may be sent and summed in bfloat16 or wider, within the bound.
A program may use at most 128 MiB of HBM per device.

```python
import math
import jax
import jax.numpy as jnp
import numpy as np
from jax import lax

HEADS = 16
HD = 128
T_DEV = 512
TOKENS = 2048
PAIRS = 1024
CLUSTERS = 8
SLOT_PAIRS = 96
N_SEQ = 4


def draw_queries(key, part):
    key = jax.random.fold_in(key, 17)
    base_draw = jax.random.normal(key, (TOKENS, HEADS * HD), jnp.float32)
    return jnp.clip(base_draw, -6.0, 6.0).astype(jnp.bfloat16)


def draw_keys(key, part):
    key = jax.random.fold_in(key, 29)
    base_draw = jax.random.normal(key, (TOKENS, HEADS * HD), jnp.float32)
    return jnp.clip(base_draw, -6.0, 6.0).astype(jnp.bfloat16)


def steps_of(rng, extent, shards, least, high):
    def one(axis_at, shards_of):
        steps = jax.random.uniform(jax.random.fold_in(jax.random.fold_in(rng, 6), axis_at), (shards_of,), jnp.float32, least / len(shards), high / len(shards))
        return jnp.repeat(jnp.exp(steps), extent[axis_at] // shards_of).reshape((-1,) + (1,) * (len(extent) - axis_at - 1))

    level = one(*shards[0])
    for cut in shards[1:]:
        level = level * one(*cut)
    return level


def routed_block(rng, own, number, rows, count, top, most, lean):
    sequence = jax.random.permutation(rng, count)
    crowded, usual = load_shares(count, rows * top, most, lean, True), load_shares(count, rows * top, most, lean, False)
    places = jnp.arange(count)

    def named(sizes, offset_by):
        used = int((sizes > 0).sum())
        fixed = max(1, used // 4)
        shifted = fixed + (places - fixed + offset_by * (used - fixed)) % max(1, count - fixed)
        return jnp.zeros((count,), jnp.int32).at[sequence[jnp.where(places < fixed, places, shifted)]].set(jnp.asarray(sizes, jnp.int32))

    sizes = jnp.where(number % 4 == 0, named(crowded, number // 4), named(usual, number - number // 4 - 1))
    mixed = jax.random.permutation(jax.random.fold_in(own, 3), count)
    giver, taker = mixed[0:count // 2 * 2:2], mixed[1:count // 2 * 2:2]
    margin = jnp.minimum(sizes[giver] - 1, most - sizes[taker]) // 2
    margin = jnp.where((giver == sequence[0]) | (taker == sequence[0]) | (sizes[taker] == 0), 0, jnp.maximum(margin, 0))
    shifted = jax.random.randint(jax.random.fold_in(own, 4), (count // 2,), 0, 1 << 20) % (margin + 1)
    sizes = sizes.at[giver].add(-shifted).at[taker].add(shifted)
    members = jnp.searchsorted(jnp.cumsum(sizes), jnp.arange(rows * top), side="right").astype(jnp.int32)
    grid = members.reshape(top, rows).T
    grid = grid[jax.random.permutation(jax.random.fold_in(own, 1), rows)]
    offset_by = jax.random.randint(jax.random.fold_in(own, 2), (rows, 1), 0, top)
    return jnp.take_along_axis(grid, (jnp.arange(top)[None, :] + offset_by) % top, axis=1)


def load_shares(number_of, total, bound, lean, full):
    portions = [(1 << 20) // math.isqrt(grade ** lean) + 1 for grade in range(1, number_of + 1)]
    largest = bound if full else min(bound, max(-(-total // number_of), total * portions[0] // sum(portions)))
    least = 1 if total - largest >= number_of - 1 else 0
    given, rest = [largest] + [least] * (number_of - 1), total - largest - least * (number_of - 1)
    while rest > 0:
        free = [i for i in range(1, number_of) if given[i] < largest] or [i for i in range(1, number_of) if given[i] < bound]
        pool, remaining = sum([portions[i] for i in free]), rest
        for i in free:
            extra = min(bound - given[i], max(1, remaining * portions[i] // pool), rest)
            given[i] = given[i] + extra
            rest = rest - extra
    return np.array(given)


def scatter_about(own_key, dims, width, reach, shards=(), kind=jnp.bfloat16):
    values = jax.random.normal(own_key, dims, jnp.float32) * width
    if len(shards) > 0:
        values = steps_of(own_key, dims, shards, -0.22, 0.18) * values
    return jnp.clip(values, min=-reach, max=reach).astype(kind)


def setup_inputs(seed: int = 0, part: int = 0) -> dict:
    seeds = jax.random.split(jax.random.key(seed), 7)
    part_splits = jax.random.split(jax.random.fold_in(seeds[6], part), 7)
    queries = draw_queries(jax.random.fold_in(jax.random.fold_in(seeds[6], part), 71), part)
    keys = draw_keys(jax.random.fold_in(jax.random.fold_in(seeds[6], part), 71), part)
    values = scatter_about(part_splits[2], (TOKENS, HEADS * HD), 1.0, 6.0, ((0, 4), (1, 4)))
    cotangent = scatter_about(part_splits[3], (TOKENS, HEADS * HD), 1.0, 6.0, ((0, 4), (1, 4)))
    cluster_ids_keys = jax.random.split(jax.random.fold_in(part_splits[4], 1), PAIRS // (T_DEV // 2))
    cluster_ids_turns = jax.random.permutation(jax.random.fold_in(part_splits[4], 3), PAIRS // (T_DEV // 2))
    cluster_ids = jax.vmap(lambda own, number: routed_block(jax.random.fold_in(part_splits[4], 2), own, number, T_DEV // 2, CLUSTERS, 1, SLOT_PAIRS, 2))(cluster_ids_keys, cluster_ids_turns).reshape((PAIRS, 1))
    centroids = scatter_about(seeds[5], (CLUSTERS, HEADS * HD), 0.1, 0.6, ((1, 4),), jnp.float32)
    return dict(queries=queries, keys=keys, values=values, cotangent=cotangent, cluster_ids=cluster_ids, centroids=centroids)


def bf16_round(array_in):
    return lax.optimization_barrier(array_in.astype(jnp.bfloat16)).astype(jnp.float32)

def reference(queries, keys, values, cotangent, cluster_ids, centroids):
    token_cluster = jnp.repeat(cluster_ids[:, 0], 2).astype(jnp.int32)
    tokens = token_cluster.shape[0]
    feature_width = HEADS * HD
    capacity = N_SEQ * 2 * SLOT_PAIRS
    score_scale = 1.0 / math.sqrt(HD)
    member = token_cluster[:, None] == jnp.arange(CLUSTERS, dtype=jnp.int32)[None, :]
    counts = lax.optimization_barrier(jnp.sum(member.astype(jnp.int32), axis=0)).astype(jnp.int32)
    starts = (jnp.cumsum(counts) - counts).astype(jnp.int32)
    sort_order = jnp.argsort(token_cluster, stable=True).astype(jnp.int32)
    sorted_cluster = token_cluster[sort_order]
    ranking = (jnp.arange(tokens, dtype=jnp.int32) - starts[sorted_cluster]).astype(jnp.int32)
    slot_table = jnp.full((CLUSTERS, capacity), tokens, jnp.int32).at[sorted_cluster, ranking].set(sort_order)
    zero_row = jnp.zeros((1, feature_width), queries.dtype)
    stacked = jnp.stack([jnp.concatenate([queries, zero_row]), jnp.concatenate([keys, zero_row]), jnp.concatenate([values, zero_row]), jnp.concatenate([cotangent, zero_row])])
    row_ids = lax.broadcasted_iota(jnp.int32, (capacity, capacity), 0)
    col_ids = lax.broadcasted_iota(jnp.int32, (capacity, capacity), 1)

    def visit_cluster(results, index_row):
        validity = index_row < tokens
        picked = stacked[:, index_row].astype(jnp.float32).reshape(4, capacity, HEADS, HD)
        query_rows, key_rows, value_rows, grad_rows = (picked[0], picked[1], picked[2], picked[3])
        allowed = (validity[:, None] & validity[None, :] & (col_ids <= row_ids) | (col_ids == row_ids))[None]
        logits = jnp.einsum('rhd,chd->hrc', query_rows, key_rows) * score_scale
        highest = lax.optimization_barrier(jnp.max(jnp.where(allowed, logits, -jnp.inf), axis=2, keepdims=True))
        lifted = jnp.where(allowed, jnp.exp(logits - highest), 0.0)
        chances = lifted / lax.optimization_barrier(jnp.sum(lifted, axis=2, keepdims=True))
        rounded = bf16_round(chances)
        attended = bf16_round(jnp.einsum('hrc,chd->rhd', rounded, value_rows))
        out_dot = lax.optimization_barrier(jnp.sum(grad_rows * attended, axis=2))
        grad_values = jnp.einsum('hrc,rhd->chd', rounded, grad_rows)
        grad_prob = jnp.einsum('rhd,chd->hrc', grad_rows, value_rows)
        grad_score = bf16_round(chances * (grad_prob - out_dot.T[:, :, None]) * score_scale)
        grad_queries = jnp.einsum('hrc,chd->rhd', grad_score, key_rows)
        grad_keys = jnp.einsum('hrc,rhd->chd', grad_score, query_rows)
        cluster_block = jnp.stack([attended, grad_queries, grad_keys, grad_values])
        cluster_block = cluster_block.reshape(4, capacity, feature_width).astype(jnp.bfloat16)
        return (results.at[:, index_row].set(cluster_block), None)
    results = jnp.zeros((4, tokens + 1, feature_width), jnp.bfloat16)
    results, _ = lax.scan(visit_cluster, results, slot_table)
    totals = jnp.dot(member.astype(jnp.bfloat16).T, queries, preferred_element_type=jnp.float32)
    blended = 0.5 * centroids + 0.5 * totals / counts.astype(jnp.float32)[:, None]
    shaped = blended.reshape(CLUSTERS, HEADS, HD)
    normed = shaped / jnp.sqrt(lax.optimization_barrier(jnp.mean(shaped * shaped, axis=2, keepdims=True)) + 1e-06)
    new_centroids = normed.reshape(CLUSTERS, feature_width)
    return (results[0, :tokens], results[1, :tokens], results[2, :tokens], results[3, :tokens], new_centroids)
```

```python
import functools
import math

import jax
import jax.numpy as jnp
from jax import lax
from jax.experimental import pallas as pl
from jax.experimental.pallas import tpu as pltpu
from jax.sharding import PartitionSpec as P

HD = 128
LANES = 128
MESH = pl.DeviceIdType.MESH
FAR = 131072.0
NT = (((1,), (1,)), ((), ()))


def product(a, b):
    return jnp.dot(a, b, preferred_element_type=jnp.float32)


def product_nt(a, b):
    return lax.dot_general(a, b, NT, preferred_element_type=jnp.float32)


def dense_kernel(
    n, clusters, tile,
    q_hbm, k_hbm, v_hbm, g_hbm, ids_ref, cent_ref,
    out_ref, dq_ref, dk_ref, dv_ref, newc_ref,
    qbuf, kbuf, vbuf, gbuf, idbuf, totbuf, statbuf, member, apart,
    m_ref, l_ref, d_ref, acc, acc2,
    own_sem, up_send, up_recv, down_send, down_recv,
    id_send, id_recv, tot_send, tot_recv, stat_send, stat_recv,
):
    tokens, width = q_hbm.shape
    heads = width // HD
    tiles = tokens // tile
    scale = 1.0 / math.sqrt(HD)
    fold = scale * math.log2(math.e)
    z = lax.axis_index("seq")

    barrier = pltpu.get_barrier_semaphore()
    for d in range(1, n):
        pl.semaphore_signal(
            barrier, inc=1, device_id={"seq": lax.rem(z + d, n)}, device_id_type=MESH
        )

    up_bufs, down_bufs = (kbuf, vbuf), (qbuf, gbuf)
    up_src, down_src = (k_hbm, v_hbm), (q_hbm, g_hbm)
    own = [
        pltpu.make_async_copy(src, buf.at[z], own_sem.at[at])
        for at, (src, buf) in enumerate(zip(up_src + down_src, up_bufs + down_bufs))
    ]
    for copy in own:
        copy.start()
    idbuf[z] = ids_ref[...]

    def up_copy(kind, age, target):
        block = z - age
        src = up_src[kind] if age == 0 else up_bufs[kind].at[block]
        return pltpu.make_async_remote_copy(
            src_ref=src, dst_ref=up_bufs[kind].at[block],
            send_sem=up_send.at[kind, age], recv_sem=up_recv.at[kind, age],
            device_id={"seq": target}, device_id_type=MESH,
        )

    def down_copy(kind, age, target):
        block = z + age
        src = down_src[kind] if age == 0 else down_bufs[kind].at[block]
        return pltpu.make_async_remote_copy(
            src_ref=src, dst_ref=down_bufs[kind].at[block],
            send_sem=down_send.at[kind, age], recv_sem=down_recv.at[kind, age],
            device_id={"seq": target}, device_id_type=MESH,
        )

    def landed(bufs, sems, kind, age, block, target):
        pltpu.make_async_remote_copy(
            src_ref=bufs[kind].at[block], dst_ref=bufs[kind].at[block],
            send_sem=sems.at[kind, age], recv_sem=sems.at[kind, age],
            device_id={"seq": target}, device_id_type=MESH,
        ).wait_recv()

    def small_copy(buf, send, recv, d, slot):
        return pltpu.make_async_remote_copy(
            src_ref=buf.at[slot], dst_ref=buf.at[slot],
            send_sem=send.at[d - 1], recv_sem=recv.at[d - 1],
            device_id={"seq": lax.rem(z + d, n)}, device_id_type=MESH,
        )

    pl.semaphore_wait(barrier, n - 1)
    for d in range(1, n):
        small_copy(idbuf, id_send, id_recv, d, z).start()
    for kind in range(2):
        @pl.when(z < n - 1)
        def _():
            up_copy(kind, 0, z + 1).start()

        @pl.when(z > 0)
        def _():
            down_copy(kind, 0, z - 1).start()

    def spread_ids(block):
        row = idbuf[block][0:1, :]
        one_hot = (
            lax.broadcasted_iota(jnp.int32, (LANES, tokens), 0).astype(jnp.float32) == row
        ).astype(jnp.float32)
        turned = one_hot.T
        member[block] = turned.astype(jnp.bfloat16)
        apart[block] = ((turned - 1.0) * FAR).astype(jnp.bfloat16)
        return jnp.sum(one_hot, axis=1, keepdims=True)[0:clusters], one_hot[0:clusters]

    counts, own_hot = spread_ids(z)
    for copy in own:
        copy.wait()
    totbuf[z] = product(own_hot.astype(jnp.bfloat16), qbuf[z])
    for d in range(1, n):
        small_copy(totbuf, tot_send, tot_recv, d, z).start()

    def place(step):
        h = step // tiles
        r = step % tiles
        return (
            h,
            r,
            pl.ds(pl.multiple_of(r * tile, tile), tile),
            pl.ds(pl.multiple_of(h * HD, HD), HD),
        )

    def later(r):
        row = lax.broadcasted_iota(jnp.int32, (tile, tokens), 0) + r * tile
        col = lax.broadcasted_iota(jnp.int32, (tile, tokens), 1)
        return row, col

    def row_scores(block, rows, cols):
        left = jnp.concatenate([qbuf[z, rows, cols], member[z, rows, :]], axis=1)
        right = jnp.concatenate([kbuf[block, :, cols], apart[block]], axis=1)
        return product_nt(left, right) * fold

    def forward(block, diagonal):
        @pl.loop(0, heads * tiles)
        def _(step):
            h, r, rows, cols = place(step)
            s = row_scores(block, rows, cols)
            if diagonal:
                row, col = later(r)
                s = jnp.where(col > row, -FAR, s)
                top = jnp.max(s, axis=1, keepdims=True)
                p = jnp.exp2(s - top)
                l_ref[h, rows, :] = jnp.sum(p, axis=1, keepdims=True)
                acc[rows, cols] = product(p.astype(jnp.bfloat16), vbuf[block, :, cols])
            else:
                old = m_ref[h, rows, :]
                top = jnp.maximum(old, jnp.max(s, axis=1, keepdims=True))
                p = jnp.exp2(s - top)
                shrink = jnp.exp2(old - top)
                l_ref[h, rows, :] = l_ref[h, rows, :] * shrink + jnp.sum(p, axis=1, keepdims=True)
                acc[rows, cols] = acc[rows, cols] * shrink + product(
                    p.astype(jnp.bfloat16), vbuf[block, :, cols]
                )
            m_ref[h, rows, :] = top

    def row_gradient(block, diagonal):
        @pl.loop(0, heads * tiles)
        def _(step):
            h, r, rows, cols = place(step)
            s = row_scores(block, rows, cols) - m_ref[h, rows, :]
            if diagonal:
                row, col = later(r)
                s = jnp.where(col > row, -FAR, s)
            p = jnp.exp2(s)
            dp = product_nt(gbuf[z, rows, cols], vbuf[block, :, cols])
            ds = (p * (dp - d_ref[h, rows, :]) * scale).astype(jnp.bfloat16)
            change = product(ds, kbuf[block, :, cols])
            if diagonal:
                acc[rows, cols] = change
            else:
                acc[rows, cols] += change

    def column_gradient(block, diagonal):
        @pl.loop(0, heads * tiles)
        def _(step):
            h, r, rows, cols = place(step)
            left = jnp.concatenate([kbuf[z, rows, cols], apart[z, rows, :]], axis=1)
            right = jnp.concatenate([qbuf[block, :, cols], member[block]], axis=1)
            s = product_nt(left, right) * fold - statbuf[block, pl.ds(h, 1), :]
            if diagonal:
                row, col = later(r)
                s = jnp.where(row > col, -FAR, s)
            p = jnp.exp2(s)
            grad = gbuf[block, :, cols]
            dv = product(p.astype(jnp.bfloat16), grad)
            dp = product_nt(vbuf[z, rows, cols], grad)
            ds = (p * (dp - statbuf[block, pl.ds(heads + h, 1), :]) * scale).astype(jnp.bfloat16)
            dk = product(ds, qbuf[block, :, cols])
            if diagonal:
                acc2[0, rows, cols] = dv
                acc2[1, rows, cols] = dk
            else:
                acc2[0, rows, cols] += dv
                acc2[1, rows, cols] += dk

    def finish_rows():
        lane = lax.broadcasted_iota(jnp.int32, (tokens, LANES), 1)
        table = jnp.zeros((tokens, LANES), jnp.float32)
        for h in range(heads):
            cols = slice(h * HD, (h + 1) * HD)
            total = l_ref[h]
            attended = (acc[:, cols] / total).astype(jnp.bfloat16)
            out_ref[:, cols] = attended
            dot = jnp.sum(
                gbuf[z, :, cols].astype(jnp.float32) * attended.astype(jnp.float32),
                axis=1, keepdims=True,
            )
            level = m_ref[h] + jnp.log2(total)
            m_ref[h] = level
            d_ref[h] = dot
            table = jnp.where(lane == h, level, table)
            table = jnp.where(lane == heads + h, dot, table)
        statbuf[z] = table.T[0 : statbuf.shape[1]]

    def stat_copy(d):
        return pltpu.make_async_remote_copy(
            src_ref=statbuf.at[z], dst_ref=statbuf.at[z],
            send_sem=stat_send.at[d - 1], recv_sem=stat_recv.at[d - 1],
            device_id={"seq": z - d}, device_id_type=MESH,
        )

    def complete():
        finish_rows()
        for d in range(1, n):
            @pl.when(z >= d)
            def _():
                stat_copy(d).start()
        row_gradient(z, True)

        @pl.loop(1, z + 1)
        def _(age):
            row_gradient(z - age, False)

        column_gradient(z, True)

    def column_turn(g):
        pltpu.make_async_remote_copy(
            src_ref=statbuf.at[z + g], dst_ref=statbuf.at[z + g],
            send_sem=stat_send.at[g - 1], recv_sem=stat_recv.at[g - 1],
            device_id={"seq": z + g}, device_id_type=MESH,
        ).wait_recv()
        column_gradient(z + g, False)

    forward(z, True)
    for d in range(1, n):
        source = lax.rem(z + n - d, n)
        small_copy(idbuf, id_send, id_recv, d, source).wait_recv()
        small_copy(totbuf, tot_send, tot_recv, d, source).wait_recv()
        other, _ = spread_ids(source)
        counts = counts + other
    totals = totbuf[0]
    for j in range(1, n):
        totals = totals + totbuf[j]
    blended = 0.5 * cent_ref[...] + 0.5 * totals / counts
    for h in range(heads):
        part = blended[:, h * HD : (h + 1) * HD]
        newc_ref[:, h * HD : (h + 1) * HD] = part * lax.rsqrt(
            jnp.mean(part * part, axis=1, keepdims=True) + 1e-06
        )

    pl.when(z == 0)(complete)
    for g in range(1, n):
        for kind in range(2):
            @pl.when(z >= g)
            def _():
                landed(up_bufs, up_recv, kind, g - 1, z - g, z - 1)

                @pl.when(z < n - 1)
                def _():
                    up_copy(kind, g, z + 1).start()

            @pl.when(z + g < n)
            def _():
                landed(down_bufs, down_recv, kind, g - 1, z + g, z + 1)

                @pl.when(z > 0)
                def _():
                    down_copy(kind, g, z - 1).start()

        @pl.when(z >= g)
        def _():
            forward(z - g, False)

        pl.when(z == g)(complete)

        @pl.when(z == 0)
        def _():
            column_turn(g)
    for g in range(1, n - 1):
        @pl.when((z > 0) & (z + g < n))
        def _():
            column_turn(g)

    dq_ref[...] = acc[...].astype(jnp.bfloat16)
    dv_ref[...] = acc2[0].astype(jnp.bfloat16)
    dk_ref[...] = acc2[1].astype(jnp.bfloat16)

    for d in range(1, n):
        small_copy(idbuf, id_send, id_recv, d, z).wait_send()
        small_copy(totbuf, tot_send, tot_recv, d, z).wait_send()

        @pl.when(z >= d)
        def _():
            stat_copy(d).wait_send()
    for age in range(n - 1):
        for kind in range(2):
            @pl.when((z >= age) & (z < n - 1))
            def _():
                up_copy(kind, age, z + 1).wait_send()

            @pl.when((z + age < n) & (z > 0))
            def _():
                down_copy(kind, age, z - 1).wait_send()


def dense_body(queries, keys, values, cotangent, cluster_ids, centroids):
    n = lax.axis_size("seq")
    tokens, width = queries.shape
    clusters = centroids.shape[0]
    heads = width // HD
    tile = min(256, tokens)
    stat_rows = -(-2 * heads // 8) * 8
    ids = jnp.broadcast_to(
        jnp.repeat(cluster_ids[:, 0], 2).astype(jnp.float32)[None, :], (8, tokens)
    )
    block = (n, tokens, width)
    act = jax.ShapeDtypeStruct((tokens, width), jnp.bfloat16)
    vmem = pl.BlockSpec(memory_space=pltpu.VMEM)
    hbm = pl.BlockSpec(memory_space=pl.ANY)
    dma = pltpu.SemaphoreType.DMA
    return pl.pallas_call(
        functools.partial(dense_kernel, n, clusters, tile),
        out_shape=[act] * 4 + [jax.ShapeDtypeStruct((clusters, width), jnp.float32)],
        in_specs=[hbm] * 4 + [vmem] * 2,
        out_specs=[vmem] * 5,
        scratch_shapes=[
            pltpu.VMEM(block, jnp.bfloat16),
            pltpu.VMEM(block, jnp.bfloat16),
            pltpu.VMEM(block, jnp.bfloat16),
            pltpu.VMEM(block, jnp.bfloat16),
            pltpu.VMEM((n, 8, tokens), jnp.float32),
            pltpu.VMEM((n, clusters, width), jnp.float32),
            pltpu.VMEM((n, stat_rows, tokens), jnp.float32),
            pltpu.VMEM((n, tokens, LANES), jnp.bfloat16),
            pltpu.VMEM((n, tokens, LANES), jnp.bfloat16),
            pltpu.VMEM((heads, tokens, 1), jnp.float32),
            pltpu.VMEM((heads, tokens, 1), jnp.float32),
            pltpu.VMEM((heads, tokens, 1), jnp.float32),
            pltpu.VMEM((tokens, width), jnp.float32),
            pltpu.VMEM((2, tokens, width), jnp.float32),
            dma((4,)),
            dma((2, n - 1)),
            dma((2, n - 1)),
            dma((2, n - 1)),
            dma((2, n - 1)),
            dma((n - 1,)),
            dma((n - 1,)),
            dma((n - 1,)),
            dma((n - 1,)),
            dma((n - 1,)),
            dma((n - 1,)),
        ],
        compiler_params=pltpu.CompilerParams(
            collective_id=0, has_side_effects=True, vmem_limit_bytes=48 * 1024 * 1024
        ),
    )(queries, keys, values, cotangent, ids, centroids)


def dispatch(stacked, slot_index, clusters, sources, slot_size):
    stack_size, tokens, feature_width = stacked.shape
    buffer = jnp.zeros((stack_size, clusters * slot_size, feature_width), stacked.dtype)
    buffer = buffer.at[:, slot_index, :].set(stacked)
    return buffer.reshape(stack_size, clusters // sources, sources, slot_size, feature_width)


def to_rows(block_data, head_count):
    item_count, sources, slot_size, feature_width = block_data.shape
    return block_data.reshape(
        item_count, sources * slot_size, head_count, feature_width // head_count
    )


def from_rows(row_data, sources):
    item_count, row_count, head_count, head_size = row_data.shape
    return row_data.reshape(item_count, sources, row_count // sources, head_count * head_size)


def live_mask(tallies, slot_size):
    count_table = tallies[0].astype(jnp.float32)
    item_count, sources = count_table.shape
    slot_place = jnp.arange(slot_size, dtype=jnp.float32)
    validity = (slot_place[None, None, :] < count_table[:, :, None]).reshape(
        item_count, sources * slot_size
    )
    row_count = sources * slot_size
    row_ids = lax.broadcasted_iota(jnp.int32, (row_count, row_count), 0)
    col_ids = lax.broadcasted_iota(jnp.int32, (row_count, row_count), 1)
    allowed = (
        validity[:, :, None] & validity[:, None, :] & (col_ids <= row_ids)[None]
        | (col_ids == row_ids)[None]
    )
    return allowed[:, None]


def probabilities(query_rows, key_rows, allowed, score_scale):
    logits = (
        jnp.einsum("irhd,ichd->ihrc", query_rows, key_rows, preferred_element_type=jnp.float32)
        * score_scale
    )
    highest = jnp.max(jnp.where(allowed, logits, -jnp.inf), axis=3, keepdims=True)
    lifted = jnp.where(allowed, jnp.exp(logits - highest), 0.0)
    chances = lifted / jnp.sum(lifted, axis=3, keepdims=True)
    return (chances, chances.astype(jnp.bfloat16))


def attend(rounded, value_rows):
    mixed_rows = jnp.einsum(
        "ihrc,ichd->irhd", rounded, value_rows, preferred_element_type=jnp.float32
    )
    return mixed_rows.astype(jnp.bfloat16)


def differentiate(
    chances, rounded, query_rows, key_rows, value_rows, grad_rows, attended, score_scale
):
    out_dot = jnp.sum(grad_rows.astype(jnp.float32) * attended.astype(jnp.float32), axis=3)
    grad_values = jnp.einsum(
        "ihrc,irhd->ichd", rounded, grad_rows, preferred_element_type=jnp.float32
    )
    grad_prob = jnp.einsum(
        "irhd,ichd->ihrc", grad_rows, value_rows, preferred_element_type=jnp.float32
    )
    grad_score = (
        chances * (grad_prob - out_dot.transpose(0, 2, 1)[..., None]) * score_scale
    ).astype(jnp.bfloat16)
    grad_queries = jnp.einsum(
        "ihrc,ichd->irhd", grad_score, key_rows, preferred_element_type=jnp.float32
    )
    grad_keys = jnp.einsum(
        "ihrc,irhd->ichd", grad_score, query_rows, preferred_element_type=jnp.float32
    )
    return (
        grad_queries.astype(jnp.bfloat16),
        grad_keys.astype(jnp.bfloat16),
        grad_values.astype(jnp.bfloat16),
    )


def renew(centroids, totals, tallies, head_count):
    blended = 0.5 * centroids + 0.5 * totals / tallies[:, None]
    shaped = blended.reshape(blended.shape[0], head_count, -1)
    normed = shaped * lax.rsqrt(jnp.mean(shaped * shaped, axis=2, keepdims=True) + 1e-06)
    return normed.reshape(blended.shape)


def dispatch_body(queries, keys, values, cotangent, cluster_ids, centroids):
    sources = lax.axis_size("seq")
    tokens, feature_width = queries.shape
    clusters = centroids.shape[0]
    owned_count = clusters // sources
    head_count = feature_width // HD
    slot_size = 2 * (3 * tokens // (2 * clusters))
    score_scale = 1.0 / math.sqrt(HD)
    token_cluster = jnp.repeat(cluster_ids[:, 0], 2)
    member = (token_cluster[:, None] == lax.broadcasted_iota(jnp.int32, (1, clusters), 1)).astype(
        jnp.bfloat16
    )
    row_ids = lax.broadcasted_iota(jnp.int32, (tokens, tokens), 0)
    col_ids = lax.broadcasted_iota(jnp.int32, (tokens, tokens), 1)
    earlier = (col_ids < row_ids).astype(jnp.bfloat16)
    before = jnp.dot(earlier, member, preferred_element_type=jnp.float32)
    ranking = jnp.sum(before * member, axis=1).astype(jnp.int32)
    owner_place = token_cluster // owned_count
    item_place = token_cluster % owned_count
    slot_index = (item_place * sources + owner_place) * slot_size + ranking
    local_counts = jnp.sum(member, axis=0, dtype=jnp.float32)
    sent_counts = local_counts.astype(jnp.bfloat16).reshape(sources, owned_count).T[None]
    outgoing = dispatch(
        jnp.stack([queries, keys, values]), slot_index, clusters, sources, slot_size
    )
    payload, tallies = (
        lax.all_to_all(outgoing, "seq", split_axis=2, concat_axis=2, tiled=True),
        lax.all_to_all(sent_counts, "seq", split_axis=2, concat_axis=2, tiled=True),
    )
    allowed = live_mask(tallies, slot_size)
    query_rows = to_rows(payload[0], head_count)
    key_rows = to_rows(payload[1], head_count)
    value_rows = to_rows(payload[2], head_count)
    chances, rounded = probabilities(query_rows, key_rows, allowed, score_scale)
    attended = attend(rounded, value_rows)
    owner_side = payload.shape[2]
    returned_out = lax.all_to_all(
        from_rows(attended, owner_side)[None], "seq", split_axis=2, concat_axis=2, tiled=True
    )
    grad_outgoing = dispatch(cotangent[None], slot_index, clusters, sources, slot_size)
    grad_payload = lax.all_to_all(grad_outgoing, "seq", split_axis=2, concat_axis=2, tiled=True)
    grad_rows = to_rows(grad_payload[0], head_count)
    grads = differentiate(
        chances, rounded, query_rows, key_rows, value_rows, grad_rows, attended, score_scale
    )
    grad_stack = jnp.stack([from_rows(part_rows, owner_side) for part_rows in grads])
    returned_grads = lax.all_to_all(grad_stack, "seq", split_axis=2, concat_axis=2, tiled=True)
    returned = jnp.concatenate([returned_out, returned_grads])
    gathered = returned.reshape(4, clusters * slot_size, feature_width)[:, slot_index, :]
    local_totals = lax.dot_general(
        member, queries, (((0,), (0,)), ((), ())), preferred_element_type=jnp.float32
    )
    totals, all_counts = (
        lax.psum(local_totals.astype(jnp.bfloat16), "seq").astype(jnp.float32),
        lax.psum(local_counts.astype(jnp.bfloat16), "seq").astype(jnp.float32),
    )
    new_centroids = renew(centroids, totals, all_counts, head_count)
    return (gathered[0], gathered[1], gathered[2], gathered[3], new_centroids)


def body(queries, keys, values, cotangent, cluster_ids, centroids):
    sources = lax.axis_size("seq")
    tokens = queries.shape[0]
    clusters = centroids.shape[0]
    slot_size = 2 * (3 * tokens // (2 * clusters))
    clustered_work = clusters // sources * (sources * slot_size) ** 2
    dense_work = sources * tokens * tokens
    chosen = dense_body if dense_work <= clustered_work else dispatch_body
    return chosen(queries, keys, values, cotangent, cluster_ids, centroids)


def solution(mesh):
    in_specs = (
        P(("groups", "seq"), "head"),
        P(("groups", "seq"), "head"),
        P(("groups", "seq"), "head"),
        P(("groups", "seq"), "head"),
        P(("groups", "seq"), None),
        P(None, "head"),
    )
    out_specs = (
        P(("groups", "seq"), "head"),
        P(("groups", "seq"), "head"),
        P(("groups", "seq"), "head"),
        P(("groups", "seq"), "head"),
        P("groups", "head"),
    )
    return jax.shard_map(body, mesh=mesh, in_specs=in_specs, out_specs=out_specs, check_vma=False)
```

```python
import functools
import math

import jax
import jax.numpy as jnp
from jax import lax
from jax.experimental import pallas as pl
from jax.experimental.pallas import tpu as pltpu
from jax.sharding import PartitionSpec as P

HD = 128
LANES = 128
MESH = pl.DeviceIdType.MESH
FAR = 131072.0
NT = (((1,), (1,)), ((), ()))
TN = (((0,), (0,)), ((), ()))


def product(a, b):
    return jnp.dot(a, b, preferred_element_type=jnp.float32)


def product_nt(a, b):
    return lax.dot_general(a, b, NT, preferred_element_type=jnp.float32)


def dense_kernel(
    n, clusters, tile,
    q_hbm, k_hbm, v_hbm, g_hbm, ids_ref, cent_ref,
    out_ref, dq_ref, dk_ref, dv_ref, newc_ref,
    qbuf, kbuf, vbuf, gbuf, idbuf, totbuf, levbuf, statbuf, member, apart, kept_p, kept_d,
    m_ref, l_ref, d_ref, acc, acc2,
    own_sem, up_send, up_recv, down_send, down_recv,
    id_send, id_recv, tot_send, tot_recv, lev_send, lev_recv, stat_send, stat_recv,
):
    tokens, width = q_hbm.shape
    heads = width // HD
    tiles = tokens // tile
    scale = 1.0 / math.sqrt(HD)
    fold = scale * math.log2(math.e)
    z = lax.axis_index("seq")

    barrier = pltpu.get_barrier_semaphore()
    for d in range(1, n):
        pl.semaphore_signal(
            barrier, inc=1, device_id={"seq": lax.rem(z + d, n)}, device_id_type=MESH
        )

    up_bufs, down_bufs = (kbuf, vbuf), (qbuf, gbuf)
    up_src, down_src = (k_hbm, v_hbm), (q_hbm, g_hbm)
    own = [
        pltpu.make_async_copy(src, buf.at[z], own_sem.at[at])
        for at, (src, buf) in enumerate(zip(up_src + down_src, up_bufs + down_bufs))
    ]
    for copy in own:
        copy.start()
    idbuf[z] = ids_ref[...]

    def up_copy(kind, age, target):
        block = z - age
        src = up_src[kind] if age == 0 else up_bufs[kind].at[block]
        return pltpu.make_async_remote_copy(
            src_ref=src, dst_ref=up_bufs[kind].at[block],
            send_sem=up_send.at[kind, age], recv_sem=up_recv.at[kind, age],
            device_id={"seq": target}, device_id_type=MESH,
        )

    def down_copy(kind, age, target):
        block = z + age
        src = down_src[kind] if age == 0 else down_bufs[kind].at[block]
        return pltpu.make_async_remote_copy(
            src_ref=src, dst_ref=down_bufs[kind].at[block],
            send_sem=down_send.at[kind, age], recv_sem=down_recv.at[kind, age],
            device_id={"seq": target}, device_id_type=MESH,
        )

    def landed(bufs, sems, kind, age, block, target):
        pltpu.make_async_remote_copy(
            src_ref=bufs[kind].at[block], dst_ref=bufs[kind].at[block],
            send_sem=sems.at[kind, age], recv_sem=sems.at[kind, age],
            device_id={"seq": target}, device_id_type=MESH,
        ).wait_recv()

    def small_copy(buf, send, recv, d, slot):
        return pltpu.make_async_remote_copy(
            src_ref=buf.at[slot], dst_ref=buf.at[slot],
            send_sem=send.at[d - 1], recv_sem=recv.at[d - 1],
            device_id={"seq": lax.rem(z + d, n)}, device_id_type=MESH,
        )

    pl.semaphore_wait(barrier, n - 1)
    for d in range(1, n):
        small_copy(idbuf, id_send, id_recv, d, z).start()
    @pl.when(z < n - 1)
    def _():
        up_copy(0, 0, z + 1).start()

    @pl.when(z > 0)
    def _():
        down_copy(0, 0, z - 1).start()

    @pl.when(z == 0)
    def _():
        up_copy(1, 0, z + 1).start()

    @pl.when(z == n - 1)
    def _():
        down_copy(1, 0, z - 1).start()

    def spread_ids(block):
        row = idbuf[block][0:1, :]
        one_hot = (
            lax.broadcasted_iota(jnp.int32, (LANES, tokens), 0).astype(jnp.float32) == row
        ).astype(jnp.float32)
        turned = one_hot.T
        member[block] = turned.astype(jnp.bfloat16)
        apart[block] = ((turned - 1.0) * FAR).astype(jnp.bfloat16)
        return jnp.sum(one_hot, axis=1, keepdims=True)[0:clusters], one_hot[0:clusters]

    counts, own_hot = spread_ids(z)
    for copy in own:
        copy.wait()
    totbuf[z] = product(own_hot.astype(jnp.bfloat16), qbuf[z])
    for d in range(1, n):
        small_copy(totbuf, tot_send, tot_recv, d, z).start()

    def place(step):
        h = step // tiles
        r = step % tiles
        return (
            h,
            r,
            pl.ds(pl.multiple_of(r * tile, tile), tile),
            pl.ds(pl.multiple_of(h * HD, HD), HD),
        )

    def later(r):
        row = lax.broadcasted_iota(jnp.int32, (tile, tokens), 0) + r * tile
        col = lax.broadcasted_iota(jnp.int32, (tile, tokens), 1)
        return row, col

    def row_scores(block, rows, cols):
        left = jnp.concatenate([qbuf[z, rows, cols], member[z, rows, :]], axis=1)
        right = jnp.concatenate([kbuf[block, :, cols], apart[block]], axis=1)
        return product_nt(left, right) * fold

    def wide(h):
        return pl.ds(pl.multiple_of(h * tokens, tokens), tokens)

    def score(block, diagonal):
        @pl.loop(0, heads * tiles)
        def _(step):
            h, r, rows, cols = place(step)
            s = row_scores(block, rows, cols)
            if diagonal:
                row, col = later(r)
                s = jnp.where(col > row, -FAR, s)
                top = jnp.max(s, axis=1, keepdims=True)
                l_ref[h, rows, :] = jnp.sum(jnp.exp2(s - top), axis=1, keepdims=True)
            else:
                old = m_ref[h, rows, :]
                top = jnp.maximum(old, jnp.max(s, axis=1, keepdims=True))
                l_ref[h, rows, :] = l_ref[h, rows, :] * jnp.exp2(old - top) + jnp.sum(
                    jnp.exp2(s - top), axis=1, keepdims=True
                )
            m_ref[h, rows, :] = top
            kept_p[block, rows, wide(h)] = s

    def normalise(block):
        @pl.loop(0, heads * tiles)
        def _(step):
            h, r, rows, cols = place(step)
            kept_p[block, rows, wide(h)] = jnp.exp2(
                kept_p[block, rows, wide(h)] - m_ref[h, rows, :]
            )

    def attend_block(block, diagonal):
        @pl.loop(0, heads * tiles)
        def _(step):
            h, r, rows, cols = place(step)
            value = vbuf[block, :, cols]
            grad = gbuf[z, rows, cols]
            p = kept_p[block, rows, wide(h)].astype(jnp.bfloat16)
            change = product(p, value)
            kept_d[block, rows, wide(h)] = product_nt(grad, value)
            if diagonal:
                acc[rows, cols] = change
                acc2[0, :, cols] += lax.dot_general(
                    p, grad, TN, preferred_element_type=jnp.float32
                )
            else:
                acc[rows, cols] += change

    def row_gradient(block, diagonal):
        @pl.loop(0, heads * tiles)
        def _(step):
            h, r, rows, cols = place(step)
            p = kept_p[block, rows, wide(h)]
            dp = kept_d[block, rows, wide(h)]
            ds = (p * (dp - d_ref[h, rows, :]) * scale).astype(jnp.bfloat16)
            change = product(ds, kbuf[block, :, cols])
            if diagonal:
                acc[rows, cols] = change
                acc2[1, :, cols] += lax.dot_general(
                    ds, qbuf[z, rows, cols], TN, preferred_element_type=jnp.float32
                )
            else:
                acc[rows, cols] += change

    def column_gradient(block):
        @pl.loop(0, heads * tiles)
        def _(step):
            h, r, rows, cols = place(step)
            left = jnp.concatenate([kbuf[z, rows, cols], apart[z, rows, :]], axis=1)
            right = jnp.concatenate([qbuf[block, :, cols], member[block]], axis=1)
            s = product_nt(left, right) * fold - levbuf[block, pl.ds(h, 1), :]
            p = jnp.exp2(s)
            grad = gbuf[block, :, cols]
            dv = product(p.astype(jnp.bfloat16), grad)
            dp = product_nt(vbuf[z, rows, cols], grad)
            ds = (p * (dp - statbuf[block, pl.ds(h, 1), :]) * scale).astype(jnp.bfloat16)
            dk = product(ds, qbuf[block, :, cols])
            acc2[0, rows, cols] += dv
            acc2[1, rows, cols] += dk

    def down_small(buf, send, recv, d, slot, target):
        return pltpu.make_async_remote_copy(
            src_ref=buf.at[slot], dst_ref=buf.at[slot],
            send_sem=send.at[d - 1], recv_sem=recv.at[d - 1],
            device_id={"seq": target}, device_id_type=MESH,
        )

    def tell_lower(buf, send, recv):
        for d in range(1, n):
            @pl.when(z >= d)
            def _():
                down_small(buf, send, recv, d, z, z - d).start()

    def finish_scores():
        lane = lax.broadcasted_iota(jnp.int32, (tokens, LANES), 1)
        table = jnp.zeros((tokens, LANES), jnp.float32)
        for h in range(heads):
            level = m_ref[h] + jnp.log2(l_ref[h])
            m_ref[h] = level
            table = jnp.where(lane == h, level, table)
        levbuf[z] = table.T[0 : levbuf.shape[1]]
        tell_lower(levbuf, lev_send, lev_recv)

        @pl.loop(0, z + 1)
        def _(age):
            normalise(z - age)

    def complete():
        lane = lax.broadcasted_iota(jnp.int32, (tokens, LANES), 1)
        table = jnp.zeros((tokens, LANES), jnp.float32)
        for h in range(heads):
            cols = slice(h * HD, (h + 1) * HD)
            attended = acc[:, cols].astype(jnp.bfloat16)
            out_ref[:, cols] = attended
            dot = jnp.sum(
                gbuf[z, :, cols].astype(jnp.float32) * attended.astype(jnp.float32),
                axis=1, keepdims=True,
            )
            d_ref[h] = dot
            table = jnp.where(lane == h, dot, table)
        statbuf[z] = table.T[0 : statbuf.shape[1]]
        tell_lower(statbuf, stat_send, stat_recv)
        row_gradient(z, True)

        @pl.loop(1, z + 1)
        def _(age):
            row_gradient(z - age, False)

    def column_turn(g):
        down_small(levbuf, lev_send, lev_recv, g, z + g, z + g).wait_recv()
        down_small(statbuf, stat_send, stat_recv, g, z + g, z + g).wait_recv()
        column_gradient(z + g)

    acc2[...] = jnp.zeros_like(acc2)
    score(z, True)
    for d in range(1, n):
        source = lax.rem(z + n - d, n)
        small_copy(idbuf, id_send, id_recv, d, source).wait_recv()
        small_copy(totbuf, tot_send, tot_recv, d, source).wait_recv()
        other, _ = spread_ids(source)
        counts = counts + other
    totals = totbuf[0]
    for j in range(1, n):
        totals = totals + totbuf[j]
    blended = 0.5 * cent_ref[...] + 0.5 * totals / counts
    for h in range(heads):
        part = blended[:, h * HD : (h + 1) * HD]
        newc_ref[:, h * HD : (h + 1) * HD] = part * lax.rsqrt(
            jnp.mean(part * part, axis=1, keepdims=True) + 1e-06
        )

    def pass_on(kind, g, seen_up, seen_down):
        @pl.when(z >= g)
        def _():
            landed(up_bufs, up_recv, kind, g - 1, z - g, z - 1)

            @pl.when(z < n - 1)
            def _():
                up_copy(kind, g, z + 1).start()

        if seen_up:
            @pl.when((z == g) & (z < n - 1))
            def _():
                up_copy(1, 0, z + 1).start()

        @pl.when(z + g < n)
        def _():
            landed(down_bufs, down_recv, kind, g - 1, z + g, z + 1)

            @pl.when(z > 0)
            def _():
                down_copy(kind, g, z - 1).start()

        if seen_down:
            @pl.when((z + g == n - 1) & (z > 0))
            def _():
                down_copy(1, 0, z - 1).start()

    pl.when(z == 0)(finish_scores)
    for g in range(1, n):
        pass_on(0, g, True, True)

        @pl.when(z >= g)
        def _():
            score(z - g, False)

        pl.when(z == g)(finish_scores)
    attend_block(z, True)
    pl.when(z == 0)(complete)
    for g in range(1, n):
        pass_on(1, g, False, False)

        @pl.when(z >= g)
        def _():
            attend_block(z - g, False)

        pl.when(z == g)(complete)

        @pl.when(z == 0)
        def _():
            column_turn(g)
    for g in range(1, n - 1):
        @pl.when((z > 0) & (z + g < n))
        def _():
            column_turn(g)

    dq_ref[...] = acc[...].astype(jnp.bfloat16)
    dv_ref[...] = acc2[0].astype(jnp.bfloat16)
    dk_ref[...] = acc2[1].astype(jnp.bfloat16)

    for d in range(1, n):
        small_copy(idbuf, id_send, id_recv, d, z).wait_send()
        small_copy(totbuf, tot_send, tot_recv, d, z).wait_send()

        @pl.when(z >= d)
        def _():
            down_small(levbuf, lev_send, lev_recv, d, z, z - d).wait_send()
            down_small(statbuf, stat_send, stat_recv, d, z, z - d).wait_send()
    for age in range(n - 1):
        for kind in range(2):
            @pl.when((z >= age) & (z < n - 1))
            def _():
                up_copy(kind, age, z + 1).wait_send()

            @pl.when((z + age < n) & (z > 0))
            def _():
                down_copy(kind, age, z - 1).wait_send()


def dense_body(queries, keys, values, cotangent, cluster_ids, centroids):
    n = lax.axis_size("seq")
    tokens, width = queries.shape
    clusters = centroids.shape[0]
    heads = width // HD
    tile = min(256, tokens)
    stat_rows = -(-heads // 8) * 8
    ids = jnp.broadcast_to(
        jnp.repeat(cluster_ids[:, 0], 2).astype(jnp.float32)[None, :], (8, tokens)
    )
    block = (n, tokens, width)
    act = jax.ShapeDtypeStruct((tokens, width), jnp.bfloat16)
    vmem = pl.BlockSpec(memory_space=pltpu.VMEM)
    hbm = pl.BlockSpec(memory_space=pltpu.HBM)
    dma = pltpu.SemaphoreType.DMA
    return pl.pallas_call(
        functools.partial(dense_kernel, n, clusters, tile),
        out_shape=[act] * 4 + [jax.ShapeDtypeStruct((clusters, width), jnp.float32)],
        in_specs=[hbm] * 4 + [vmem] * 2,
        out_specs=[vmem] * 5,
        scratch_shapes=[
            pltpu.VMEM(block, jnp.bfloat16),
            pltpu.VMEM(block, jnp.bfloat16),
            pltpu.VMEM(block, jnp.bfloat16),
            pltpu.VMEM(block, jnp.bfloat16),
            pltpu.VMEM((n, 8, tokens), jnp.float32),
            pltpu.VMEM((n, clusters, width), jnp.float32),
            pltpu.VMEM((n, stat_rows, tokens), jnp.float32),
            pltpu.VMEM((n, stat_rows, tokens), jnp.float32),
            pltpu.VMEM((n, tokens, LANES), jnp.bfloat16),
            pltpu.VMEM((n, tokens, LANES), jnp.bfloat16),
            pltpu.VMEM((n, tokens, heads * tokens), jnp.float32),
            pltpu.VMEM((n, tokens, heads * tokens), jnp.float32),
            pltpu.VMEM((heads, tokens, 1), jnp.float32),
            pltpu.VMEM((heads, tokens, 1), jnp.float32),
            pltpu.VMEM((heads, tokens, 1), jnp.float32),
            pltpu.VMEM((tokens, width), jnp.float32),
            pltpu.VMEM((2, tokens, width), jnp.float32),
            dma((4,)),
            dma((2, n - 1)),
            dma((2, n - 1)),
            dma((2, n - 1)),
            dma((2, n - 1)),
            dma((n - 1,)),
            dma((n - 1,)),
            dma((n - 1,)),
            dma((n - 1,)),
            dma((n - 1,)),
            dma((n - 1,)),
            dma((n - 1,)),
            dma((n - 1,)),
        ],
        compiler_params=pltpu.CompilerParams(
            collective_id=0, has_side_effects=True, vmem_limit_bytes=60 * 1024 * 1024
        ),
    )(queries, keys, values, cotangent, ids, centroids)


def dispatch(stacked, slot_index, clusters, sources, slot_size):
    stack_size, tokens, feature_width = stacked.shape
    buffer = jnp.zeros((stack_size, clusters * slot_size, feature_width), stacked.dtype)
    buffer = buffer.at[:, slot_index, :].set(stacked)
    return buffer.reshape(stack_size, clusters // sources, sources, slot_size, feature_width)


def to_rows(block_data, head_count):
    item_count, sources, slot_size, feature_width = block_data.shape
    return block_data.reshape(
        item_count, sources * slot_size, head_count, feature_width // head_count
    )


def from_rows(row_data, sources):
    item_count, row_count, head_count, head_size = row_data.shape
    return row_data.reshape(item_count, sources, row_count // sources, head_count * head_size)


def live_mask(tallies, slot_size):
    count_table = tallies[0].astype(jnp.float32)
    item_count, sources = count_table.shape
    slot_place = jnp.arange(slot_size, dtype=jnp.float32)
    validity = (slot_place[None, None, :] < count_table[:, :, None]).reshape(
        item_count, sources * slot_size
    )
    row_count = sources * slot_size
    row_ids = lax.broadcasted_iota(jnp.int32, (row_count, row_count), 0)
    col_ids = lax.broadcasted_iota(jnp.int32, (row_count, row_count), 1)
    allowed = (
        validity[:, :, None] & validity[:, None, :] & (col_ids <= row_ids)[None]
        | (col_ids == row_ids)[None]
    )
    return allowed[:, None]


def probabilities(query_rows, key_rows, allowed, score_scale):
    logits = (
        jnp.einsum("irhd,ichd->ihrc", query_rows, key_rows, preferred_element_type=jnp.float32)
        * score_scale
    )
    highest = jnp.max(jnp.where(allowed, logits, -jnp.inf), axis=3, keepdims=True)
    lifted = jnp.where(allowed, jnp.exp(logits - highest), 0.0)
    chances = lifted / jnp.sum(lifted, axis=3, keepdims=True)
    return (chances, chances.astype(jnp.bfloat16))


def attend(rounded, value_rows):
    mixed_rows = jnp.einsum(
        "ihrc,ichd->irhd", rounded, value_rows, preferred_element_type=jnp.float32
    )
    return mixed_rows.astype(jnp.bfloat16)


def differentiate(
    chances, rounded, query_rows, key_rows, value_rows, grad_rows, attended, score_scale
):
    out_dot = jnp.sum(grad_rows.astype(jnp.float32) * attended.astype(jnp.float32), axis=3)
    grad_values = jnp.einsum(
        "ihrc,irhd->ichd", rounded, grad_rows, preferred_element_type=jnp.float32
    )
    grad_prob = jnp.einsum(
        "irhd,ichd->ihrc", grad_rows, value_rows, preferred_element_type=jnp.float32
    )
    grad_score = (
        chances * (grad_prob - out_dot.transpose(0, 2, 1)[..., None]) * score_scale
    ).astype(jnp.bfloat16)
    grad_queries = jnp.einsum(
        "ihrc,ichd->irhd", grad_score, key_rows, preferred_element_type=jnp.float32
    )
    grad_keys = jnp.einsum(
        "ihrc,irhd->ichd", grad_score, query_rows, preferred_element_type=jnp.float32
    )
    return (
        grad_queries.astype(jnp.bfloat16),
        grad_keys.astype(jnp.bfloat16),
        grad_values.astype(jnp.bfloat16),
    )


def renew(centroids, totals, tallies, head_count):
    blended = 0.5 * centroids + 0.5 * totals / tallies[:, None]
    shaped = blended.reshape(blended.shape[0], head_count, -1)
    normed = shaped * lax.rsqrt(jnp.mean(shaped * shaped, axis=2, keepdims=True) + 1e-06)
    return normed.reshape(blended.shape)


def dispatch_body(queries, keys, values, cotangent, cluster_ids, centroids):
    sources = lax.axis_size("seq")
    tokens, feature_width = queries.shape
    clusters = centroids.shape[0]
    owned_count = clusters // sources
    head_count = feature_width // HD
    slot_size = 2 * (3 * tokens // (2 * clusters))
    score_scale = 1.0 / math.sqrt(HD)
    token_cluster = jnp.repeat(cluster_ids[:, 0], 2)
    member = (token_cluster[:, None] == lax.broadcasted_iota(jnp.int32, (1, clusters), 1)).astype(
        jnp.bfloat16
    )
    row_ids = lax.broadcasted_iota(jnp.int32, (tokens, tokens), 0)
    col_ids = lax.broadcasted_iota(jnp.int32, (tokens, tokens), 1)
    earlier = (col_ids < row_ids).astype(jnp.bfloat16)
    before = jnp.dot(earlier, member, preferred_element_type=jnp.float32)
    ranking = jnp.sum(before * member, axis=1).astype(jnp.int32)
    owner_place = token_cluster // owned_count
    item_place = token_cluster % owned_count
    slot_index = (item_place * sources + owner_place) * slot_size + ranking
    local_counts = jnp.sum(member, axis=0, dtype=jnp.float32)
    sent_counts = local_counts.astype(jnp.bfloat16).reshape(sources, owned_count).T[None]
    outgoing = dispatch(
        jnp.stack([queries, keys, values]), slot_index, clusters, sources, slot_size
    )
    payload, tallies = (
        lax.all_to_all(outgoing, "seq", split_axis=2, concat_axis=2, tiled=True),
        lax.all_to_all(sent_counts, "seq", split_axis=2, concat_axis=2, tiled=True),
    )
    allowed = live_mask(tallies, slot_size)
    query_rows = to_rows(payload[0], head_count)
    key_rows = to_rows(payload[1], head_count)
    value_rows = to_rows(payload[2], head_count)
    chances, rounded = probabilities(query_rows, key_rows, allowed, score_scale)
    attended = attend(rounded, value_rows)
    owner_side = payload.shape[2]
    returned_out = lax.all_to_all(
        from_rows(attended, owner_side)[None], "seq", split_axis=2, concat_axis=2, tiled=True
    )
    grad_outgoing = dispatch(cotangent[None], slot_index, clusters, sources, slot_size)
    grad_payload = lax.all_to_all(grad_outgoing, "seq", split_axis=2, concat_axis=2, tiled=True)
    grad_rows = to_rows(grad_payload[0], head_count)
    grads = differentiate(
        chances, rounded, query_rows, key_rows, value_rows, grad_rows, attended, score_scale
    )
    grad_stack = jnp.stack([from_rows(part_rows, owner_side) for part_rows in grads])
    returned_grads = lax.all_to_all(grad_stack, "seq", split_axis=2, concat_axis=2, tiled=True)
    returned = jnp.concatenate([returned_out, returned_grads])
    gathered = returned.reshape(4, clusters * slot_size, feature_width)[:, slot_index, :]
    local_totals = lax.dot_general(
        member, queries, (((0,), (0,)), ((), ())), preferred_element_type=jnp.float32
    )
    totals, all_counts = (
        lax.psum(local_totals.astype(jnp.bfloat16), "seq").astype(jnp.float32),
        lax.psum(local_counts.astype(jnp.bfloat16), "seq").astype(jnp.float32),
    )
    new_centroids = renew(centroids, totals, all_counts, head_count)
    return (gathered[0], gathered[1], gathered[2], gathered[3], new_centroids)


def body(queries, keys, values, cotangent, cluster_ids, centroids):
    sources = lax.axis_size("seq")
    tokens = queries.shape[0]
    clusters = centroids.shape[0]
    slot_size = 2 * (3 * tokens // (2 * clusters))
    clustered_work = clusters // sources * (sources * slot_size) ** 2
    dense_work = sources * tokens * tokens
    chosen = dense_body if dense_work <= clustered_work else dispatch_body
    return chosen(queries, keys, values, cotangent, cluster_ids, centroids)


def solution(mesh):
    in_specs = (
        P(("groups", "seq"), "head"),
        P(("groups", "seq"), "head"),
        P(("groups", "seq"), "head"),
        P(("groups", "seq"), "head"),
        P(("groups", "seq"), None),
        P(None, "head"),
    )
    out_specs = (
        P(("groups", "seq"), "head"),
        P(("groups", "seq"), "head"),
        P(("groups", "seq"), "head"),
        P(("groups", "seq"), "head"),
        P("groups", "head"),
    )
    return jax.shard_map(body, mesh=mesh, in_specs=in_specs, out_specs=out_specs, check_vma=False)
```

```python
import functools
import math

import jax
import jax.numpy as jnp
from jax import lax
from jax.experimental import pallas as pl
from jax.experimental.pallas import tpu as pltpu
from jax.sharding import PartitionSpec as P

HD = 128
LANES = 128
MESH = pl.DeviceIdType.MESH
FAR = 131072.0
NT = (((1,), (1,)), ((), ()))
TN = (((0,), (0,)), ((), ()))


def product(a, b):
    return jnp.dot(a, b, preferred_element_type=jnp.float32)


def product_nt(a, b):
    return lax.dot_general(a, b, NT, preferred_element_type=jnp.float32)


def dense_kernel(
    n, clusters, tile,
    q_hbm, k_hbm, v_hbm, g_hbm, ids_ref, cent_ref,
    out_ref, dq_ref, dk_ref, dv_ref, newc_ref,
    qbuf, kbuf, vbuf, gbuf, idbuf, totbuf, levbuf, statbuf, member, apart, kept_p, kept_d,
    m_ref, l_ref, d_ref, acc, acc2,
    own_sem, up_send, up_recv, down_send, down_recv,
    id_send, id_recv, tot_send, tot_recv, lev_send, lev_recv, stat_send, stat_recv,
):
    tokens, width = q_hbm.shape
    heads = width // HD
    tiles = tokens // tile
    scale = 1.0 / math.sqrt(HD)
    fold = scale * math.log2(math.e)
    z = lax.axis_index("seq")

    barrier = pltpu.get_barrier_semaphore()
    for d in range(1, n):
        pl.semaphore_signal(
            barrier, inc=1, device_id={"seq": lax.rem(z + d, n)}, device_id_type=MESH
        )

    up_bufs, down_bufs = (kbuf, vbuf), (qbuf, gbuf)
    up_src, down_src = (k_hbm, v_hbm), (q_hbm, g_hbm)
    own = [
        pltpu.make_async_copy(src, buf.at[z], own_sem.at[at])
        for at, (src, buf) in enumerate(zip(up_src + down_src, up_bufs + down_bufs))
    ]
    for copy in own:
        copy.start()
    idbuf[z] = ids_ref[...]

    def up_copy(kind, age, target):
        block = z - age
        src = up_src[kind] if age == 0 else up_bufs[kind].at[block]
        return pltpu.make_async_remote_copy(
            src_ref=src, dst_ref=up_bufs[kind].at[block],
            send_sem=up_send.at[kind, age], recv_sem=up_recv.at[kind, age],
            device_id={"seq": target}, device_id_type=MESH,
        )

    def down_copy(kind, age, target):
        block = z + age
        src = down_src[kind] if age == 0 else down_bufs[kind].at[block]
        return pltpu.make_async_remote_copy(
            src_ref=src, dst_ref=down_bufs[kind].at[block],
            send_sem=down_send.at[kind, age], recv_sem=down_recv.at[kind, age],
            device_id={"seq": target}, device_id_type=MESH,
        )

    def landed(bufs, sems, kind, age, block, target):
        pltpu.make_async_remote_copy(
            src_ref=bufs[kind].at[block], dst_ref=bufs[kind].at[block],
            send_sem=sems.at[kind, age], recv_sem=sems.at[kind, age],
            device_id={"seq": target}, device_id_type=MESH,
        ).wait_recv()

    def small_copy(buf, send, recv, d, slot):
        return pltpu.make_async_remote_copy(
            src_ref=buf.at[slot], dst_ref=buf.at[slot],
            send_sem=send.at[d - 1], recv_sem=recv.at[d - 1],
            device_id={"seq": lax.rem(z + d, n)}, device_id_type=MESH,
        )

    pl.semaphore_wait(barrier, n - 1)
    for d in range(1, n):
        small_copy(idbuf, id_send, id_recv, d, z).start()
    for kind in range(2):
        @pl.when(z < n - 1)
        def _():
            up_copy(kind, 0, z + 1).start()

        @pl.when(z > 0)
        def _():
            down_copy(kind, 0, z - 1).start()

    def spread_ids(block):
        row = idbuf[block][0:1, :]
        one_hot = (
            lax.broadcasted_iota(jnp.int32, (LANES, tokens), 0).astype(jnp.float32) == row
        ).astype(jnp.float32)
        turned = one_hot.T
        member[block] = turned.astype(jnp.bfloat16)
        apart[block] = ((turned - 1.0) * FAR).astype(jnp.bfloat16)
        return jnp.sum(one_hot, axis=1, keepdims=True)[0:clusters], one_hot[0:clusters]

    counts, own_hot = spread_ids(z)
    for copy in own:
        copy.wait()
    totbuf[z] = product(own_hot.astype(jnp.bfloat16), qbuf[z])
    for d in range(1, n):
        small_copy(totbuf, tot_send, tot_recv, d, z).start()

    def place(step):
        h = step // tiles
        r = step % tiles
        return (
            h,
            r,
            pl.ds(pl.multiple_of(r * tile, tile), tile),
            pl.ds(pl.multiple_of(h * HD, HD), HD),
        )

    def later(r):
        row = lax.broadcasted_iota(jnp.int32, (tile, tokens), 0) + r * tile
        col = lax.broadcasted_iota(jnp.int32, (tile, tokens), 1)
        return row, col

    def row_scores(block, rows, cols):
        left = jnp.concatenate([qbuf[z, rows, cols], member[z, rows, :]], axis=1)
        right = jnp.concatenate([kbuf[block, :, cols], apart[block]], axis=1)
        return product_nt(left, right) * fold

    def wide(h):
        return pl.ds(pl.multiple_of(h * tokens, tokens), tokens)

    def score(block, diagonal):
        @pl.loop(0, heads * tiles)
        def _(step):
            h, r, rows, cols = place(step)
            s = row_scores(block, rows, cols)
            if diagonal:
                row, col = later(r)
                s = jnp.where(col > row, -FAR, s)
                top = jnp.max(s, axis=1, keepdims=True)
                l_ref[h, rows, :] = jnp.sum(jnp.exp2(s - top), axis=1, keepdims=True)
            else:
                old = m_ref[h, rows, :]
                top = jnp.maximum(old, jnp.max(s, axis=1, keepdims=True))
                l_ref[h, rows, :] = l_ref[h, rows, :] * jnp.exp2(old - top) + jnp.sum(
                    jnp.exp2(s - top), axis=1, keepdims=True
                )
            m_ref[h, rows, :] = top
            kept_p[block, rows, wide(h)] = s

    def normalise(block):
        @pl.loop(0, heads * tiles)
        def _(step):
            h, r, rows, cols = place(step)
            kept_p[block, rows, wide(h)] = jnp.exp2(
                kept_p[block, rows, wide(h)] - m_ref[h, rows, :]
            )

    def attend_block(block, diagonal):
        @pl.loop(0, heads * tiles)
        def _(step):
            h, r, rows, cols = place(step)
            value = vbuf[block, :, cols]
            grad = gbuf[z, rows, cols]
            p = kept_p[block, rows, wide(h)].astype(jnp.bfloat16)
            change = product(p, value)
            kept_d[block, rows, wide(h)] = product_nt(grad, value)
            if diagonal:
                acc[rows, cols] = change
                acc2[0, :, cols] += lax.dot_general(
                    p, grad, TN, preferred_element_type=jnp.float32
                )
            else:
                acc[rows, cols] += change

    def row_gradient(block, diagonal):
        @pl.loop(0, heads * tiles)
        def _(step):
            h, r, rows, cols = place(step)
            p = kept_p[block, rows, wide(h)]
            dp = kept_d[block, rows, wide(h)]
            ds = (p * (dp - d_ref[h, rows, :]) * scale).astype(jnp.bfloat16)
            change = product(ds, kbuf[block, :, cols])
            if diagonal:
                acc[rows, cols] = change
                acc2[1, :, cols] += lax.dot_general(
                    ds, qbuf[z, rows, cols], TN, preferred_element_type=jnp.float32
                )
            else:
                acc[rows, cols] += change

    def column_gradient(block):
        @pl.loop(0, heads * tiles)
        def _(step):
            h, r, rows, cols = place(step)
            left = jnp.concatenate([kbuf[z, rows, cols], apart[z, rows, :]], axis=1)
            right = jnp.concatenate([qbuf[block, :, cols], member[block]], axis=1)
            s = product_nt(left, right) * fold - levbuf[block, pl.ds(h, 1), :]
            p = jnp.exp2(s)
            grad = gbuf[block, :, cols]
            dv = product(p.astype(jnp.bfloat16), grad)
            dp = product_nt(vbuf[z, rows, cols], grad)
            ds = (p * (dp - statbuf[block, pl.ds(h, 1), :]) * scale).astype(jnp.bfloat16)
            dk = product(ds, qbuf[block, :, cols])
            acc2[0, rows, cols] += dv
            acc2[1, rows, cols] += dk

    def down_small(buf, send, recv, d, slot, target):
        return pltpu.make_async_remote_copy(
            src_ref=buf.at[slot], dst_ref=buf.at[slot],
            send_sem=send.at[d - 1], recv_sem=recv.at[d - 1],
            device_id={"seq": target}, device_id_type=MESH,
        )

    def tell_lower(buf, send, recv):
        for d in range(1, n):
            @pl.when(z >= d)
            def _():
                down_small(buf, send, recv, d, z, z - d).start()

    def finish_scores():
        lane = lax.broadcasted_iota(jnp.int32, (tokens, LANES), 1)
        table = jnp.zeros((tokens, LANES), jnp.float32)
        for h in range(heads):
            level = m_ref[h] + jnp.log2(l_ref[h])
            m_ref[h] = level
            table = jnp.where(lane == h, level, table)
        levbuf[z] = table.T[0 : levbuf.shape[1]]
        tell_lower(levbuf, lev_send, lev_recv)

        @pl.loop(0, z + 1)
        def _(age):
            normalise(z - age)

    def complete():
        lane = lax.broadcasted_iota(jnp.int32, (tokens, LANES), 1)
        table = jnp.zeros((tokens, LANES), jnp.float32)
        for h in range(heads):
            cols = slice(h * HD, (h + 1) * HD)
            attended = acc[:, cols].astype(jnp.bfloat16)
            out_ref[:, cols] = attended
            dot = jnp.sum(
                gbuf[z, :, cols].astype(jnp.float32) * attended.astype(jnp.float32),
                axis=1, keepdims=True,
            )
            d_ref[h] = dot
            table = jnp.where(lane == h, dot, table)
        statbuf[z] = table.T[0 : statbuf.shape[1]]
        tell_lower(statbuf, stat_send, stat_recv)
        row_gradient(z, True)

        @pl.loop(1, z + 1)
        def _(age):
            row_gradient(z - age, False)

    def column_turn(g):
        down_small(levbuf, lev_send, lev_recv, g, z + g, z + g).wait_recv()
        down_small(statbuf, stat_send, stat_recv, g, z + g, z + g).wait_recv()
        column_gradient(z + g)

    acc2[...] = jnp.zeros_like(acc2)
    score(z, True)
    for d in range(1, n):
        source = lax.rem(z + n - d, n)
        small_copy(idbuf, id_send, id_recv, d, source).wait_recv()
        small_copy(totbuf, tot_send, tot_recv, d, source).wait_recv()
        other, _ = spread_ids(source)
        counts = counts + other
    totals = totbuf[0]
    for j in range(1, n):
        totals = totals + totbuf[j]
    blended = 0.5 * cent_ref[...] + 0.5 * totals / counts
    for h in range(heads):
        part = blended[:, h * HD : (h + 1) * HD]
        newc_ref[:, h * HD : (h + 1) * HD] = part * lax.rsqrt(
            jnp.mean(part * part, axis=1, keepdims=True) + 1e-06
        )

    def pass_on(kind, g):
        @pl.when(z >= g)
        def _():
            landed(up_bufs, up_recv, kind, g - 1, z - g, z - 1)

            @pl.when(z < n - 1)
            def _():
                up_copy(kind, g, z + 1).start()

        @pl.when(z + g < n)
        def _():
            landed(down_bufs, down_recv, kind, g - 1, z + g, z + 1)

            @pl.when(z > 0)
            def _():
                down_copy(kind, g, z - 1).start()

    pl.when(z == 0)(finish_scores)
    for g in range(1, n):
        pass_on(0, g)

        @pl.when(z >= g)
        def _():
            score(z - g, False)

        pl.when(z == g)(finish_scores)
    attend_block(z, True)
    pl.when(z == 0)(complete)
    for g in range(1, n):
        pass_on(1, g)

        @pl.when(z >= g)
        def _():
            attend_block(z - g, False)

        pl.when(z == g)(complete)

        @pl.when(z == 0)
        def _():
            column_turn(g)
    for g in range(1, n - 1):
        @pl.when((z > 0) & (z + g < n))
        def _():
            column_turn(g)

    dq_ref[...] = acc[...].astype(jnp.bfloat16)
    dv_ref[...] = acc2[0].astype(jnp.bfloat16)
    dk_ref[...] = acc2[1].astype(jnp.bfloat16)

    for d in range(1, n):
        small_copy(idbuf, id_send, id_recv, d, z).wait_send()
        small_copy(totbuf, tot_send, tot_recv, d, z).wait_send()

        @pl.when(z >= d)
        def _():
            down_small(levbuf, lev_send, lev_recv, d, z, z - d).wait_send()
            down_small(statbuf, stat_send, stat_recv, d, z, z - d).wait_send()
    for age in range(n - 1):
        for kind in range(2):
            @pl.when((z >= age) & (z < n - 1))
            def _():
                up_copy(kind, age, z + 1).wait_send()

            @pl.when((z + age < n) & (z > 0))
            def _():
                down_copy(kind, age, z - 1).wait_send()


def dense_body(queries, keys, values, cotangent, cluster_ids, centroids):
    n = lax.axis_size("seq")
    tokens, width = queries.shape
    clusters = centroids.shape[0]
    heads = width // HD
    tile = min(256, tokens)
    stat_rows = -(-heads // 8) * 8
    ids = jnp.broadcast_to(
        jnp.repeat(cluster_ids[:, 0], 2).astype(jnp.float32)[None, :], (8, tokens)
    )
    block = (n, tokens, width)
    act = jax.ShapeDtypeStruct((tokens, width), jnp.bfloat16)
    vmem = pl.BlockSpec(memory_space=pltpu.VMEM)
    hbm = pl.BlockSpec(memory_space=pltpu.HBM)
    dma = pltpu.SemaphoreType.DMA
    return pl.pallas_call(
        functools.partial(dense_kernel, n, clusters, tile),
        out_shape=[act] * 4 + [jax.ShapeDtypeStruct((clusters, width), jnp.float32)],
        in_specs=[hbm] * 4 + [vmem] * 2,
        out_specs=[vmem] * 5,
        scratch_shapes=[
            pltpu.VMEM(block, jnp.bfloat16),
            pltpu.VMEM(block, jnp.bfloat16),
            pltpu.VMEM(block, jnp.bfloat16),
            pltpu.VMEM(block, jnp.bfloat16),
            pltpu.VMEM((n, 8, tokens), jnp.float32),
            pltpu.VMEM((n, clusters, width), jnp.float32),
            pltpu.VMEM((n, stat_rows, tokens), jnp.float32),
            pltpu.VMEM((n, stat_rows, tokens), jnp.float32),
            pltpu.VMEM((n, tokens, LANES), jnp.bfloat16),
            pltpu.VMEM((n, tokens, LANES), jnp.bfloat16),
            pltpu.VMEM((n, tokens, heads * tokens), jnp.float32),
            pltpu.VMEM((n, tokens, heads * tokens), jnp.float32),
            pltpu.VMEM((heads, tokens, 1), jnp.float32),
            pltpu.VMEM((heads, tokens, 1), jnp.float32),
            pltpu.VMEM((heads, tokens, 1), jnp.float32),
            pltpu.VMEM((tokens, width), jnp.float32),
            pltpu.VMEM((2, tokens, width), jnp.float32),
            dma((4,)),
            dma((2, n - 1)),
            dma((2, n - 1)),
            dma((2, n - 1)),
            dma((2, n - 1)),
            dma((n - 1,)),
            dma((n - 1,)),
            dma((n - 1,)),
            dma((n - 1,)),
            dma((n - 1,)),
            dma((n - 1,)),
            dma((n - 1,)),
            dma((n - 1,)),
        ],
        compiler_params=pltpu.CompilerParams(
            collective_id=0, has_side_effects=True, vmem_limit_bytes=60 * 1024 * 1024
        ),
    )(queries, keys, values, cotangent, ids, centroids)


def dispatch(stacked, slot_index, clusters, sources, slot_size):
    stack_size, tokens, feature_width = stacked.shape
    buffer = jnp.zeros((stack_size, clusters * slot_size, feature_width), stacked.dtype)
    buffer = buffer.at[:, slot_index, :].set(stacked)
    return buffer.reshape(stack_size, clusters // sources, sources, slot_size, feature_width)


def to_rows(block_data, head_count):
    item_count, sources, slot_size, feature_width = block_data.shape
    return block_data.reshape(
        item_count, sources * slot_size, head_count, feature_width // head_count
    )


def from_rows(row_data, sources):
    item_count, row_count, head_count, head_size = row_data.shape
    return row_data.reshape(item_count, sources, row_count // sources, head_count * head_size)


def live_mask(tallies, slot_size):
    count_table = tallies[0].astype(jnp.float32)
    item_count, sources = count_table.shape
    slot_place = jnp.arange(slot_size, dtype=jnp.float32)
    validity = (slot_place[None, None, :] < count_table[:, :, None]).reshape(
        item_count, sources * slot_size
    )
    row_count = sources * slot_size
    row_ids = lax.broadcasted_iota(jnp.int32, (row_count, row_count), 0)
    col_ids = lax.broadcasted_iota(jnp.int32, (row_count, row_count), 1)
    allowed = (
        validity[:, :, None] & validity[:, None, :] & (col_ids <= row_ids)[None]
        | (col_ids == row_ids)[None]
    )
    return allowed[:, None]


def probabilities(query_rows, key_rows, allowed, score_scale):
    logits = (
        jnp.einsum("irhd,ichd->ihrc", query_rows, key_rows, preferred_element_type=jnp.float32)
        * score_scale
    )
    highest = jnp.max(jnp.where(allowed, logits, -jnp.inf), axis=3, keepdims=True)
    lifted = jnp.where(allowed, jnp.exp(logits - highest), 0.0)
    chances = lifted / jnp.sum(lifted, axis=3, keepdims=True)
    return (chances, chances.astype(jnp.bfloat16))


def attend(rounded, value_rows):
    mixed_rows = jnp.einsum(
        "ihrc,ichd->irhd", rounded, value_rows, preferred_element_type=jnp.float32
    )
    return mixed_rows.astype(jnp.bfloat16)


def differentiate(
    chances, rounded, query_rows, key_rows, value_rows, grad_rows, attended, score_scale
):
    out_dot = jnp.sum(grad_rows.astype(jnp.float32) * attended.astype(jnp.float32), axis=3)
    grad_values = jnp.einsum(
        "ihrc,irhd->ichd", rounded, grad_rows, preferred_element_type=jnp.float32
    )
    grad_prob = jnp.einsum(
        "irhd,ichd->ihrc", grad_rows, value_rows, preferred_element_type=jnp.float32
    )
    grad_score = (
        chances * (grad_prob - out_dot.transpose(0, 2, 1)[..., None]) * score_scale
    ).astype(jnp.bfloat16)
    grad_queries = jnp.einsum(
        "ihrc,ichd->irhd", grad_score, key_rows, preferred_element_type=jnp.float32
    )
    grad_keys = jnp.einsum(
        "ihrc,irhd->ichd", grad_score, query_rows, preferred_element_type=jnp.float32
    )
    return (
        grad_queries.astype(jnp.bfloat16),
        grad_keys.astype(jnp.bfloat16),
        grad_values.astype(jnp.bfloat16),
    )


def renew(centroids, totals, tallies, head_count):
    blended = 0.5 * centroids + 0.5 * totals / tallies[:, None]
    shaped = blended.reshape(blended.shape[0], head_count, -1)
    normed = shaped * lax.rsqrt(jnp.mean(shaped * shaped, axis=2, keepdims=True) + 1e-06)
    return normed.reshape(blended.shape)


def dispatch_body(queries, keys, values, cotangent, cluster_ids, centroids):
    sources = lax.axis_size("seq")
    tokens, feature_width = queries.shape
    clusters = centroids.shape[0]
    owned_count = clusters // sources
    head_count = feature_width // HD
    slot_size = 2 * (3 * tokens // (2 * clusters))
    score_scale = 1.0 / math.sqrt(HD)
    token_cluster = jnp.repeat(cluster_ids[:, 0], 2)
    member = (token_cluster[:, None] == lax.broadcasted_iota(jnp.int32, (1, clusters), 1)).astype(
        jnp.bfloat16
    )
    row_ids = lax.broadcasted_iota(jnp.int32, (tokens, tokens), 0)
    col_ids = lax.broadcasted_iota(jnp.int32, (tokens, tokens), 1)
    earlier = (col_ids < row_ids).astype(jnp.bfloat16)
    before = jnp.dot(earlier, member, preferred_element_type=jnp.float32)
    ranking = jnp.sum(before * member, axis=1).astype(jnp.int32)
    owner_place = token_cluster // owned_count
    item_place = token_cluster % owned_count
    slot_index = (item_place * sources + owner_place) * slot_size + ranking
    local_counts = jnp.sum(member, axis=0, dtype=jnp.float32)
    sent_counts = local_counts.astype(jnp.bfloat16).reshape(sources, owned_count).T[None]
    outgoing = dispatch(
        jnp.stack([queries, keys, values]), slot_index, clusters, sources, slot_size
    )
    payload, tallies = (
        lax.all_to_all(outgoing, "seq", split_axis=2, concat_axis=2, tiled=True),
        lax.all_to_all(sent_counts, "seq", split_axis=2, concat_axis=2, tiled=True),
    )
    allowed = live_mask(tallies, slot_size)
    query_rows = to_rows(payload[0], head_count)
    key_rows = to_rows(payload[1], head_count)
    value_rows = to_rows(payload[2], head_count)
    chances, rounded = probabilities(query_rows, key_rows, allowed, score_scale)
    attended = attend(rounded, value_rows)
    owner_side = payload.shape[2]
    returned_out = lax.all_to_all(
        from_rows(attended, owner_side)[None], "seq", split_axis=2, concat_axis=2, tiled=True
    )
    grad_outgoing = dispatch(cotangent[None], slot_index, clusters, sources, slot_size)
    grad_payload = lax.all_to_all(grad_outgoing, "seq", split_axis=2, concat_axis=2, tiled=True)
    grad_rows = to_rows(grad_payload[0], head_count)
    grads = differentiate(
        chances, rounded, query_rows, key_rows, value_rows, grad_rows, attended, score_scale
    )
    grad_stack = jnp.stack([from_rows(part_rows, owner_side) for part_rows in grads])
    returned_grads = lax.all_to_all(grad_stack, "seq", split_axis=2, concat_axis=2, tiled=True)
    returned = jnp.concatenate([returned_out, returned_grads])
    gathered = returned.reshape(4, clusters * slot_size, feature_width)[:, slot_index, :]
    local_totals = lax.dot_general(
        member, queries, (((0,), (0,)), ((), ())), preferred_element_type=jnp.float32
    )
    totals, all_counts = (
        lax.psum(local_totals.astype(jnp.bfloat16), "seq").astype(jnp.float32),
        lax.psum(local_counts.astype(jnp.bfloat16), "seq").astype(jnp.float32),
    )
    new_centroids = renew(centroids, totals, all_counts, head_count)
    return (gathered[0], gathered[1], gathered[2], gathered[3], new_centroids)


def body(queries, keys, values, cotangent, cluster_ids, centroids):
    sources = lax.axis_size("seq")
    tokens = queries.shape[0]
    clusters = centroids.shape[0]
    slot_size = 2 * (3 * tokens // (2 * clusters))
    clustered_work = clusters // sources * (sources * slot_size) ** 2
    dense_work = sources * tokens * tokens
    chosen = dense_body if dense_work <= clustered_work else dispatch_body
    return chosen(queries, keys, values, cotangent, cluster_ids, centroids)


def solution(mesh):
    in_specs = (
        P(("groups", "seq"), "head"),
        P(("groups", "seq"), "head"),
        P(("groups", "seq"), "head"),
        P(("groups", "seq"), "head"),
        P(("groups", "seq"), None),
        P(None, "head"),
    )
    out_specs = (
        P(("groups", "seq"), "head"),
        P(("groups", "seq"), "head"),
        P(("groups", "seq"), "head"),
        P(("groups", "seq"), "head"),
        P("groups", "head"),
    )
    return jax.shard_map(body, mesh=mesh, in_specs=in_specs, out_specs=out_specs, check_vma=False)
```
